32 devices in a mesh: expert: 16 (over z, y, x), shard: 2 (over core).
Axes of the slice: x: 2, y: 2, z: 4, core: 2. Of those that a mesh axis runs over, the one named last changes fastest.
Arguments:
- hidden_in: bfloat16 [4096, 1024], P(('expert', 'shard')), may hold values from -6 to 6
- doc_lengths: int32 [32, 3], P('expert'), may hold values from 1 to 96, 128 in all within a row
- routes: int32 [4096, 8], P(('expert', 'shard')), may hold values from 0 to 15, all different within a row; in each aligned block of 128 rows (0 to 127, 128 to 255, ...) at most 68 rows name the same one
- attn_norm_gain: float32 [1024], replicated, may hold values from 0.5 to 1.5
- query_weight: bfloat16 [1024, 1024], P('shard'), may hold values from -0.75 to 0.75
- key_weight: bfloat16 [1024, 512], P('shard'), may hold values from -0.75 to 0.75
- value_weight: bfloat16 [1024, 512], P('shard'), may hold values from -0.75 to 0.75
- output_weight: bfloat16 [1024, 1024], P('shard'), may hold values from -0.75 to 0.75
- router_weight: bfloat16 [1024, 16], P('shard'), may hold values from -0.09375 to 0.09375
- moe_norm_gain: float32 [1024], replicated, may hold values from 0.5 to 1.5
- gate_weight: bfloat16 [16, 1024, 512], P('expert'), may hold values from -0.1875 to 0.1875
- up_weight: bfloat16 [16, 1024, 512], P('expert'), may hold values from -0.75 to 0.75
- down_weight: bfloat16 [16, 512, 1024], P('expert'), may hold values from -1.5 to 1.5
- cotangent: bfloat16 [4096, 1024], P(('expert', 'shard')), may hold values from -6 to 6
Outputs:
- layer_out: bfloat16 [4096, 1024], P(('expert', 'shard'))
- input_grad: float32 [4096, 1024], P(('expert', 'shard'))
- attn_norm_grad: float32 [1024], P('shard')
- query_grad: float32 [1024, 1024], P('shard')
- key_grad: float32 [1024, 512], P('shard')
- value_grad: float32 [1024, 512], P('shard')
- output_grad: float32 [1024, 1024], P('shard')
- router_grad: float32 [1024, 16], P('shard')
- moe_norm_grad: float32 [1024], P('shard')
- gate_grad: float32 [16, 1024, 512], P('expert', 'shard')
- up_grad: float32 [16, 1024, 512], P('expert', 'shard')
- down_grad: float32 [16, 512, 1024], P('expert', 'shard')
The draws below stay inside these ranges and needn't reach their ends.
Inputs may be any that keep to these rules, and one draw needn't show every extreme that they name: `routes`: in the 128 tokens of one device no expert is named more than 68 times, a bound that some block reaches; a token names 8 different experts. `doc_lengths`: each row sums to 128; its longest document has 128 - 128 // 4 tokens.
All inputs are finite; a program needn't handle non-finite values.
Results may differ from the reference program's by a relative error of at most 0.02.
Values may be sent and summed in bfloat16 or wider, within the bound.
A program may use at most 128 MiB of HBM per device.

```python
import math
import jax
import jax.numpy as jnp
import numpy as np
from jax import lax

D = 1024
HEADS = 16
KV_HEADS = 8
HEAD_DIM = 64
FF = 512
TOP = 8
DOCS = 3
TOK_DEV = 128
EXPERTS = 16
SUB = 64
SEQ = 128
SEQS = 32
TOKENS = 4096
CAP = 68
N_EXPERT = 16
N_SHARD = 2


def levels(key, extent, shards, least, largest):
    def one(axis_at, parts):
        steps = jax.random.uniform(jax.random.fold_in(jax.random.fold_in(key, 6), axis_at), (parts,), jnp.float32, least / len(shards), largest / len(shards))
        return jnp.repeat(jnp.exp(steps), extent[axis_at] // parts).reshape((-1,) + (1,) * (len(extent) - axis_at - 1))

    level = one(*shards[0])
    for cut in shards[1:]:
        level = level * one(*cut)
    return level


def split_up(amount, total, limit, lean):
    portions = [(1 << 20) // math.isqrt(rank ** lean) + 1 for rank in range(2, amount + 1)]
    rest, counts = total - limit - (amount - 1), [1] * (amount - 1)
    while rest > 0:
        candidates = [i for i in range(amount - 1) if counts[i] < limit]
        mass, remaining = sum([portions[i] for i in candidates]), rest
        for i in candidates:
            more = min(limit - counts[i], max(1, remaining * portions[i] // mass), rest)
            counts[i] = counts[i] + more
            rest = rest - more
    return np.array([limit] + counts)


def uneven_parts(stream_key, number_of, total, most, slope):
    if number_of == 2:
        one = jax.random.randint(stream_key, (), max(1, total - most), min(most, total - 1) + 1)
        return jnp.stack([one, total - one])
    tallies = jnp.asarray(split_up(number_of, total, most, slope), jnp.int32)
    twos = (number_of - 1) // 2
    giver, sink = tallies[1:1 + 2 * twos:2], tallies[2:2 + 2 * twos:2]
    slack = jnp.minimum(giver - 1, most - sink)
    passed = jax.random.randint(jax.random.fold_in(stream_key, 1), (twos,), 0, 1 << 20) % (slack + 1)
    tallies = tallies.at[1:1 + 2 * twos:2].set(giver - passed).at[2:2 + 2 * twos:2].set(sink + passed)
    return tallies[jax.random.permutation(jax.random.fold_in(stream_key, 2), number_of)]


def assign_block(stream_key, own, number, rows, number_of, top, most, skew):
    order = jax.random.permutation(stream_key, number_of)
    packed, ordinary = portions_of(number_of, rows * top, most, skew, True), portions_of(number_of, rows * top, most, skew, False)
    places = jnp.arange(number_of)

    def named(sizes, rotation):
        used = int((sizes > 0).sum())
        fixed = max(1, used // 4)
        passed = fixed + (places - fixed + rotation * (used - fixed)) % max(1, number_of - fixed)
        return jnp.zeros((number_of,), jnp.int32).at[order[jnp.where(places < fixed, places, passed)]].set(jnp.asarray(sizes, jnp.int32))

    sizes = jnp.where(number % 4 == 0, named(packed, number // 4), named(ordinary, number - number // 4 - 1))
    mixed = jax.random.permutation(jax.random.fold_in(own, 3), number_of)
    source_of, taker = mixed[0:number_of // 2 * 2:2], mixed[1:number_of // 2 * 2:2]
    room = jnp.minimum(sizes[source_of] - 1, most - sizes[taker]) // 2
    room = jnp.where((source_of == order[0]) | (taker == order[0]) | (sizes[taker] == 0), 0, jnp.maximum(room, 0))
    passed = jax.random.randint(jax.random.fold_in(own, 4), (number_of // 2,), 0, 1 << 20) % (room + 1)
    sizes = sizes.at[source_of].add(-passed).at[taker].add(passed)
    labels = jnp.searchsorted(jnp.cumsum(sizes), jnp.arange(rows * top), side="right").astype(jnp.int32)
    grid = labels.reshape(top, rows).T
    grid = grid[jax.random.permutation(jax.random.fold_in(own, 1), rows)]
    rotation = jax.random.randint(jax.random.fold_in(own, 2), (rows, 1), 0, top)
    return jnp.take_along_axis(grid, (jnp.arange(top)[None, :] + rotation) % top, axis=1)


def portions_of(number_of, total, bound, slope, full):
    weights = [(1 << 20) // math.isqrt(grade ** slope) + 1 for grade in range(1, number_of + 1)]
    largest = bound if full else min(bound, max(-(-total // number_of), total * weights[0] // sum(weights)))
    least = 1 if total - largest >= number_of - 1 else 0
    holding, spare = [largest] + [least] * (number_of - 1), total - largest - least * (number_of - 1)
    while spare > 0:
        free = [i for i in range(1, number_of) if holding[i] < largest] or [i for i in range(1, number_of) if holding[i] < bound]
        mass, left = sum([weights[i] for i in free]), spare
        for i in free:
            addition = min(bound - holding[i], max(1, left * weights[i] // mass), spare)
            holding[i] = holding[i] + addition
            spare = spare - addition
    return np.array(holding)


def centred(rng, extent, width, most, split=(), dtype=jnp.bfloat16):
    values = width * jax.random.normal(rng, extent, jnp.float32)
    if split:
        values = values * levels(rng, extent, split, -0.22, 0.18)
    return jnp.clip(values, -most, most).astype(dtype)


def setup_inputs(seed: int = 0) -> dict:
    seeds = jax.random.split(jax.random.key(seed), 15)
    hidden_in = centred(seeds[0], (TOKENS, D), 1.0, 6.0, ((0, 32),))
    doc_lengths = jax.vmap(lambda own: uneven_parts(own, DOCS, SEQ, SEQ - TOK_DEV // 4, 0))(jax.random.split(seeds[1], SEQS)).reshape((SEQS, DOCS)).astype(jnp.int32)
    routes_keys = jax.random.split(jax.random.fold_in(seeds[2], 1), TOKENS // TOK_DEV)
    routes_turns = jax.random.permutation(jax.random.fold_in(seeds[2], 3), TOKENS // TOK_DEV)
    routes = jax.vmap(lambda own, number: assign_block(jax.random.fold_in(seeds[2], 2), own, number, TOK_DEV, EXPERTS, TOP, CAP, 1))(routes_keys, routes_turns).reshape((TOKENS, TOP))
    attn_norm_gain = jnp.clip(1.0 + 0.1 * jax.random.normal(seeds[3], (D,), jnp.float32), 0.5, 1.5)
    query_weight = centred(seeds[4], (D, HEADS * HEAD_DIM), (D // 16) ** -0.5, 0.75, ((0, 2),))
    key_weight = centred(seeds[5], (D, KV_HEADS * HEAD_DIM), (D // 16) ** -0.5, 0.75, ((0, 2),))
    value_weight = centred(seeds[6], (D, KV_HEADS * HEAD_DIM), (D // 16) ** -0.5, 0.75, ((0, 2),))
    output_weight = centred(seeds[7], (HEADS * HEAD_DIM, D), (HEADS * HEAD_DIM // 16) ** -0.5, 0.75, ((0, 2),))
    router_weight = centred(seeds[8], (D, EXPERTS), (4 * D) ** -0.5, 0.09375, ((0, 2),))
    moe_norm_gain = jnp.clip(1.0 + 0.1 * jax.random.normal(seeds[9], (D,), jnp.float32), 0.5, 1.5)
    gate_weight = centred(seeds[10], (EXPERTS, D, FF), D ** -0.5, 0.1875, ((0, 16),))
    up_weight = centred(seeds[11], (EXPERTS, D, FF), (D // 16) ** -0.5, 0.75, ((0, 16),))
    down_weight = centred(seeds[12], (EXPERTS, FF, D), (FF // 32) ** -0.5, 1.5, ((0, 16),))
    cotangent = centred(seeds[13], (TOKENS, D), 1.0, 6.0, ((0, 32),))
    return {"hidden_in": hidden_in, "doc_lengths": doc_lengths, "routes": routes, "attn_norm_gain": attn_norm_gain, "query_weight": query_weight, "key_weight": key_weight, "value_weight": value_weight, "output_weight": output_weight, "router_weight": router_weight, "moe_norm_gain": moe_norm_gain, "gate_weight": gate_weight, "up_weight": up_weight, "down_weight": down_weight, "cotangent": cotangent}


epsilon = 1e-06
res_scale = 0.22
att_scale = 0.015625
rope_base = 10000.0
masked_score = -1e+30
highest = lax.Precision.HIGHEST

@jax.custom_vjp
def low(v):
    return lax.optimization_barrier(v.astype(jnp.bfloat16)).astype(jnp.float32)

@jax.custom_vjp
def low_back(v):
    return v

def low_keep(v):
    return (low(v), None)

def low_pass(kept, grad):
    return (grad,)

def back_keep(v):
    return (v, None)

def back_low(kept, grad):
    return (low(grad),)
low.defvjp(low_keep, low_pass)
low_back.defvjp(back_keep, back_low)

def rms_norm(values, gain):
    return values * lax.rsqrt(lax.optimization_barrier(jnp.mean(values * values, -1, keepdims=True)) + epsilon) * gain

def doc_layout(lengths, positions):
    doc_ends = jnp.cumsum(lengths).astype(jnp.int32)
    past_end = positions[:, None] >= doc_ends[None, :]
    doc_index = lax.optimization_barrier(jnp.sum(past_end.astype(jnp.int32), 1)).astype(jnp.int32)
    doc_start = lax.optimization_barrier(jnp.sum(jnp.where(past_end, lengths[None, :], 0), 1)).astype(jnp.int32)
    return (doc_index, positions - doc_start)

def rope_tables(offsets):
    half_size = HEAD_DIM // 2
    frequency = rope_base ** (-2.0 * jnp.arange(half_size).astype(jnp.float32) / HEAD_DIM)
    angles = offsets.astype(jnp.float32)[:, None] * frequency[None, :]
    return (jnp.cos(angles), jnp.sin(angles))

def rotate(values, cos_table, sin_table):
    row_count = values.shape[0]
    shaped = values.reshape(row_count, -1, HEAD_DIM)
    half_size = HEAD_DIM // 2
    front_part = shaped[:, :, :half_size]
    back_part = shaped[:, :, half_size:]
    cos_wide = cos_table[:, None, :]
    sin_wide = sin_table[:, None, :]
    turned = jnp.concatenate([front_part * cos_wide - back_part * sin_wide, back_part * cos_wide + front_part * sin_wide], -1)
    return turned.reshape(row_count, -1)

def group_attention(normed, lengths, query_weight, key_weight, value_weight, output_weight):
    length = normed.shape[0]
    positions = jnp.arange(length).astype(jnp.int32)
    doc_index, offsets = doc_layout(lengths, positions)
    cos_table, sin_table = rope_tables(offsets)
    query_raw = low_back(jnp.dot(normed, query_weight, precision=highest))
    key_raw = low_back(jnp.dot(normed, key_weight, precision=highest))
    value_low = low(low_back(jnp.dot(normed, value_weight, precision=highest)))
    query_rot = low(rotate(query_raw, cos_table, sin_table))
    key_rot = low(rotate(key_raw, cos_table, sin_table))
    query_heads = query_rot.reshape(length, KV_HEADS, HEADS // KV_HEADS, HEAD_DIM)
    key_heads = key_rot.reshape(length, KV_HEADS, HEAD_DIM)
    value_heads = value_low.reshape(length, KV_HEADS, HEAD_DIM)
    scores = low_back(jnp.einsum('tkgd,skd->kgts', query_heads, key_heads, precision=highest) * att_scale)
    allowed = (positions[:, None] >= positions[None, :]) & (doc_index[:, None] == doc_index[None, :])
    scores = jnp.where(allowed, scores, masked_score)
    top_score = lax.optimization_barrier(jnp.max(scores, -1, keepdims=True))
    exp_scores = jnp.exp(scores - top_score)
    probs = low(exp_scores / lax.optimization_barrier(jnp.sum(exp_scores, -1, keepdims=True)))
    mixed = jnp.einsum('kgts,skd->tkgd', probs, value_heads, precision=highest).reshape(length, -1)
    mixed = low(low_back(mixed))
    return low_back(jnp.dot(mixed, output_weight, precision=highest))

def block_experts(normed, block_routes, block_gates, gate_weight, up_weight, down_weight):
    slot_expert = block_routes.reshape(-1)
    slot_hot = (slot_expert[:, None] == jnp.arange(EXPERTS).astype(jnp.int32)[None, :]).astype(jnp.int32)
    slot_place = lax.optimization_barrier(jnp.sum((jnp.cumsum(slot_hot, 0) - slot_hot) * slot_hot, 1)).astype(jnp.int32)
    slot_rows = low_back(jnp.repeat(normed, TOP, 0))
    buffer = jnp.zeros((EXPERTS, CAP, D), jnp.float32).at[slot_expert, slot_place].set(slot_rows)
    gate_pre = low_back(jnp.einsum('ecd,edf->ecf', buffer, gate_weight, precision=highest))
    up_pre = low_back(jnp.einsum('ecd,edf->ecf', buffer, up_weight, precision=highest))
    inner = low(jax.nn.silu(gate_pre) * up_pre)
    result = low(low_back(jnp.einsum('ecf,efd->ecd', inner, down_weight, precision=highest)))
    taken = result[slot_expert, slot_place].reshape(-1, TOP, D)
    return jnp.einsum('tj,tjd->td', block_gates, taken, precision=highest)

def forward(hidden_in, attn_norm_gain, query_weight, key_weight, value_weight, output_weight, router_weight, moe_norm_gain, gate_weight, up_weight, down_weight, doc_lengths, routes):
    normed_one = low(rms_norm(hidden_in, attn_norm_gain))

    def one_group(pair):
        return group_attention(pair[0], pair[1], query_weight, key_weight, value_weight, output_weight)
    seq_rows = normed_one.reshape(N_EXPERT, N_SHARD, 2, SUB, D).transpose(0, 2, 1, 3, 4).reshape(SEQS, SEQ, D)
    branch = lax.map(jax.checkpoint(one_group), (seq_rows, doc_lengths))
    branch = branch.reshape(N_EXPERT, 2, N_SHARD, SUB, D).transpose(0, 2, 1, 3, 4).reshape(TOKENS, D)
    middle = hidden_in + res_scale * branch
    normed_two = low(rms_norm(middle, moe_norm_gain))
    logits = low_back(jnp.dot(normed_two, router_weight, precision=highest))
    route_picks = (routes[:, :, None] == jnp.arange(EXPERTS).astype(jnp.int32)[None, None, :]).astype(jnp.float32)
    chosen = lax.optimization_barrier(jnp.sum(route_picks * logits[:, None, :], -1))
    top_chosen = lax.optimization_barrier(jnp.max(chosen, -1, keepdims=True))
    gate_exp = jnp.exp(chosen - top_chosen)
    gate_probs = gate_exp / lax.optimization_barrier(jnp.sum(gate_exp, -1, keepdims=True))
    block_count = TOKENS // TOK_DEV

    def one_block(triple):
        return block_experts(triple[0], triple[1], triple[2], gate_weight, up_weight, down_weight)
    mixture = lax.map(jax.checkpoint(one_block), (normed_two.reshape(block_count, TOK_DEV, D), routes.reshape(block_count, TOK_DEV, TOP), gate_probs.reshape(block_count, TOK_DEV, TOP)))
    return middle + res_scale * mixture.reshape(TOKENS, D)

def reference(hidden_in, doc_lengths, routes, attn_norm_gain, query_weight, key_weight, value_weight, output_weight, router_weight, moe_norm_gain, gate_weight, up_weight, down_weight, cotangent):
    float_args = (hidden_in.astype(jnp.float32), attn_norm_gain.astype(jnp.float32), query_weight.astype(jnp.float32), key_weight.astype(jnp.float32), value_weight.astype(jnp.float32), output_weight.astype(jnp.float32), router_weight.astype(jnp.float32), moe_norm_gain.astype(jnp.float32), gate_weight.astype(jnp.float32), up_weight.astype(jnp.float32), down_weight.astype(jnp.float32))

    def layer(*params):
        return forward(*params, doc_lengths, routes)
    layer_value, pull_back = jax.vjp(layer, *float_args)
    grads = pull_back(cotangent.astype(jnp.float32))
    return (layer_value.astype(jnp.bfloat16), grads[0], grads[1], grads[2], grads[3], grads[4], grads[5], grads[6], grads[7], grads[8], grads[9], grads[10])
```

```python
import functools

import jax
import jax.numpy as jnp
from jax import lax
from jax.experimental import pallas as pl
from jax.experimental.pallas import tpu as pltpu
from jax.sharding import PartitionSpec as P

HEADS = 16
KV_HEADS = 8
HEAD_DIM = 64
TOP = 8


epsilon = 1e-06
res_scale = 0.22
att_scale = 0.015625
rope_base = 10000.0
masked_score = -1e30


def rms_norm(values, gain):
    return values * lax.rsqrt(jnp.mean(values * values, -1, keepdims=True) + epsilon) * gain


def doc_layout(lengths, positions):
    doc_ends = jnp.cumsum(lengths)
    past_end = positions[:, None] >= doc_ends[None, :]
    doc_index = jnp.sum(past_end.astype(jnp.int32), 1)
    doc_start = jnp.sum(jnp.where(past_end, lengths[None, :], 0), 1)
    return (doc_index, positions - doc_start)


def rope_tables(offsets):
    half_size = HEAD_DIM // 2
    frequency = rope_base ** (-2.0 * jnp.arange(half_size).astype(jnp.float32) / HEAD_DIM)
    angles = offsets.astype(jnp.float32)[:, None] * frequency[None, :]
    return (jnp.cos(angles), jnp.sin(angles))


def rotate(values, cos_table, sin_table, inverse):
    row_count = values.shape[0]
    shaped = values.reshape(row_count, -1, HEAD_DIM)
    half_size = HEAD_DIM // 2
    front_part = shaped[:, :, :half_size]
    back_part = shaped[:, :, half_size:]
    cos_wide = cos_table[:, None, :]
    sin_wide = sin_table[:, None, :]
    if inverse:
        sin_wide = -sin_wide
    turned = jnp.concatenate(
        [
            front_part * cos_wide - back_part * sin_wide,
            back_part * cos_wide + front_part * sin_wide,
        ],
        -1,
    )
    return turned.reshape(row_count, -1)


MESH_ID = pl.DeviceIdType.MESH
vmem_grant = 48 * 1024 * 1024


def greet(devices):
    barrier = pltpu.get_barrier_semaphore()
    for device in devices:
        pl.semaphore_signal(barrier, inc=1, device_id=device, device_id_type=MESH_ID)
    pl.semaphore_wait(barrier, len(devices))


def gather_kernel(count, *refs):
    sources, results = refs[:count], refs[count : 2 * count]
    send_sem, recv_sem, own_sem = refs[2 * count :]
    expert_index, shard_index = lax.axis_index("expert"), lax.axis_index("shard")
    other = (expert_index, 1 - shard_index)
    greet([other])
    copies = []
    for at in range(count):
        copies.append(
            pltpu.make_async_remote_copy(
                src_ref=sources[at],
                dst_ref=results[at].at[shard_index],
                send_sem=send_sem.at[at],
                recv_sem=recv_sem.at[at],
                device_id=other,
                device_id_type=MESH_ID,
            )
        )
        copies.append(
            pltpu.make_async_copy(sources[at], results[at].at[shard_index], own_sem.at[at])
        )
    for copy in copies:
        copy.start()
    for copy in copies:
        copy.wait()


def gather_pair(arrays, identity):
    count = len(arrays)
    return pl.pallas_call(
        functools.partial(gather_kernel, count),
        out_shape=[jax.ShapeDtypeStruct((2,) + a.shape, a.dtype) for a in arrays],
        in_specs=[pl.BlockSpec(memory_space=pl.ANY)] * count,
        out_specs=[pl.BlockSpec(memory_space=pl.ANY)] * count,
        scratch_shapes=[pltpu.SemaphoreType.DMA((count,))] * 3,
        compiler_params=pltpu.CompilerParams(collective_id=identity, has_side_effects=True),
    )(*arrays)


def swap_kernel(source, result, send_sem, recv_sem):
    expert_index, shard_index = lax.axis_index("expert"), lax.axis_index("shard")
    other = (expert_index, 1 - shard_index)
    greet([other])
    copy = pltpu.make_async_remote_copy(
        src_ref=source.at[1 - shard_index],
        dst_ref=result,
        send_sem=send_sem,
        recv_sem=recv_sem,
        device_id=other,
        device_id_type=MESH_ID,
    )
    copy.start()
    copy.wait()


def swap_pair(array, identity):
    return pl.pallas_call(
        swap_kernel,
        out_shape=jax.ShapeDtypeStruct(array.shape[1:], array.dtype),
        in_specs=[pl.BlockSpec(memory_space=pl.ANY)],
        out_specs=pl.BlockSpec(memory_space=pl.ANY),
        scratch_shapes=[pltpu.SemaphoreType.DMA, pltpu.SemaphoreType.DMA],
        compiler_params=pltpu.CompilerParams(collective_id=identity, has_side_effects=True),
    )(array)


def add_rows(target, target_at, first, first_at, second, second_at, rows):
    step = min(rows, 32)

    def one(index, carry):
        row = index * step
        into = pl.ds(pl.multiple_of(target_at + row, step), step)
        left = pl.ds(pl.multiple_of(first_at + row, step), step)
        right = pl.ds(pl.multiple_of(second_at + row, step), step)
        total = first[left, :].astype(jnp.float32) + second[right, :].astype(jnp.float32)
        target[into, :] = total.astype(target.dtype)
        return carry

    lax.fori_loop(0, rows // step, one, 0)


def reduce_kernel(levels, parts, swaps, *refs):
    refs = list(refs)

    def take(amount):
        taken = refs[:amount]
        del refs[:amount]
        return taken

    sources, swap_sources = take(parts), take(swaps)
    totals, swap_results = take(parts), take(swaps)
    near, far, held_sums = take(parts), take(parts), take(parts)
    send_sem, recv_sem, swap_send, swap_recv = refs
    expert_index, shard_index = lax.axis_index("expert"), lax.axis_index("shard")
    other = (expert_index, 1 - shard_index)
    held = [(expert_index // (1 << bit)) % 2 for bit in range(levels)]
    partners = [
        (expert_index + (1 << bit) * (1 - 2 * held[bit]), shard_index) for bit in range(levels)
    ]
    greet([other] + partners)
    rows = totals[0].shape[0]

    def send(part, step, source, target, device):
        copy = pltpu.make_async_remote_copy(
            src_ref=source,
            dst_ref=target,
            send_sem=send_sem.at[part, step],
            recv_sem=recv_sem.at[part, step],
            device_id=device,
            device_id_type=MESH_ID,
        )
        copy.start()
        return copy

    flying = []
    for part in range(parts):
        away = pl.ds(pl.multiple_of((1 - shard_index) * rows, rows), rows)
        flying.append(send(part, 0, sources[part].at[away], near[part], other))
    swapping = []
    for at in range(swaps):
        copy = pltpu.make_async_remote_copy(
            src_ref=swap_sources[at].at[1 - shard_index],
            dst_ref=swap_results[at],
            send_sem=swap_send.at[at],
            recv_sem=swap_recv.at[at],
            device_id=other,
            device_id_type=MESH_ID,
        )
        copy.start()
        swapping.append(copy)
    starts = [0] * parts
    size = rows
    landing = 0
    for step in range(2 * levels + 1):
        for part in range(parts):
            flying[part].wait()
            if step == 0:
                add_rows(
                    held_sums[part], 0, sources[part], shard_index * rows, near[part], 0, rows
                )
            elif step <= levels:
                bit = (step - 1 + part) % levels
                starts[part] = starts[part] + held[bit] * (size // 2)
                add_rows(
                    totals[part] if step == levels else held_sums[part],
                    starts[part],
                    held_sums[part],
                    starts[part],
                    far[part],
                    landing,
                    size // 2,
                )
            else:
                bit = (2 * levels - step + part) % levels
                starts[part] = starts[part] - held[bit] * size
            if step < levels:
                half = (size if step == 0 else size // 2) // 2
                bit = (step + part) % levels
                leaving = pl.multiple_of(starts[part] + (1 - held[bit]) * half, half)
                room = 0 if step == 0 else landing + size // 2
                flying[part] = send(
                    part,
                    step + 1,
                    held_sums[part].at[pl.ds(leaving, half)],
                    far[part].at[pl.ds(room, half)],
                    partners[bit],
                )
            elif step < 2 * levels:
                whole = size // 2 if step == levels else size * 2
                bit = (2 * levels - 1 - step + part) % levels
                region = pl.ds(pl.multiple_of(starts[part], whole), whole)
                flying[part] = send(
                    part, step + 1, totals[part].at[region], totals[part].at[region], partners[bit]
                )
        if 1 <= step <= levels:
            landing += size // 2
            size //= 2
        elif step > levels:
            size *= 2
    for copy in swapping:
        copy.wait()


def reduce_all(sources, swap_sources, expert_count, identity):
    parts, swaps = len(sources), len(swap_sources)
    levels = expert_count.bit_length() - 1
    rows = sources[0].shape[0] // 2
    spec = pl.BlockSpec(memory_space=pltpu.VMEM)
    return pl.pallas_call(
        functools.partial(reduce_kernel, levels, parts, swaps),
        out_shape=[jax.ShapeDtypeStruct((rows, a.shape[1]), a.dtype) for a in sources]
        + [jax.ShapeDtypeStruct(a.shape[1:], a.dtype) for a in swap_sources],
        in_specs=[spec] * (parts + swaps),
        out_specs=[spec] * (parts + swaps),
        scratch_shapes=[pltpu.VMEM((rows, a.shape[1]), a.dtype) for a in list(sources) * 3]
        + [pltpu.SemaphoreType.DMA((parts, 2 * levels + 1))] * 2
        + [pltpu.SemaphoreType.DMA((swaps,))] * 2,
        compiler_params=pltpu.CompilerParams(
            collective_id=identity, has_side_effects=True, vmem_limit_bytes=vmem_grant
        ),
    )(*sources, *swap_sources)


def on_device(
    hidden_in,
    doc_lengths,
    routes,
    attn_norm_gain,
    query_weight,
    key_weight,
    value_weight,
    output_weight,
    router_weight,
    moe_norm_gain,
    gate_weight,
    up_weight,
    down_weight,
    cotangent,
):
    low = jnp.bfloat16
    wide = jnp.float32
    tok_count, model_width = hidden_in.shape
    shard_index = lax.axis_index("shard")
    shard_count = lax.axis_size("shard")
    expert_axis = lax.axis_size("expert")
    expert_index = lax.axis_index("expert")
    paired = shard_count == 2
    expert_count = router_weight.shape[1]
    capacity = 17 * tok_count * TOP // (16 * expert_count)
    capacity = -(-capacity // 8) * 8
    sub_rows = tok_count // 2
    seq_len = sub_rows * shard_count
    group_ratio = HEADS // KV_HEADS
    kv_width = key_weight.shape[1]

    picks = jnp.any(
        routes[:, :, None] == jnp.arange(expert_count, dtype=jnp.int32)[None, None, :], 1
    )
    picks_low = picks.astype(low)
    earlier = jnp.tril(jnp.ones((tok_count, tok_count), low), -1)
    place = jnp.dot(earlier, picks_low, preferred_element_type=wide).astype(jnp.int32)
    place = jnp.where(picks, place, -1)
    hot = (
        place.T[:, None, :] == jnp.arange(capacity, dtype=jnp.int32)[None, :, None]
    ).astype(low)
    hot = hot.reshape(expert_count * capacity, tok_count)

    def to_slots(values):
        rows = jnp.dot(hot, values, preferred_element_type=wide).astype(low)
        return rows.reshape(expert_count, capacity, -1)

    def cross(values):
        return lax.all_to_all(values, "expert", split_axis=0, concat_axis=0, tiled=True)

    picks_wide = jnp.pad(picks_low, ((0, 0), (0, -expert_count % 128)))
    arrived_top = cross(to_slots(jnp.concatenate([cotangent, picks_wide], 1)))

    router_wide = jnp.pad(router_weight, ((0, 0), (0, -expert_count % 128)))
    weights = [query_weight, key_weight, value_weight, output_weight, router_wide]
    if paired:
        gathered = [a.reshape(-1, a.shape[2]) for a in gather_pair(weights, 1)]
    else:
        gathered = [lax.all_gather(a, "shard", axis=0, tiled=True) for a in weights]
    query_full, key_full, value_full, output_full, router_padded = gathered
    router_full = router_padded[:, :expert_count]

    input_float = hidden_in.astype(wide)
    normed_one = rms_norm(input_float, attn_norm_gain).astype(low)
    query_raw = jnp.dot(normed_one, query_full, preferred_element_type=wide)
    key_raw = jnp.dot(normed_one, key_full, preferred_element_type=wide)
    value_raw = jnp.dot(normed_one, value_full, preferred_element_type=wide)
    own_positions = shard_index * sub_rows + jnp.arange(sub_rows, dtype=jnp.int32)
    seq_positions = jnp.arange(seq_len, dtype=jnp.int32)
    layout_both = jax.vmap(doc_layout, in_axes=(0, None))
    query_docs, query_offsets = layout_both(doc_lengths, own_positions)
    key_docs, unused_offsets = layout_both(doc_lengths, seq_positions)
    cos_table, sin_table = rope_tables(query_offsets.reshape(-1))
    query_rot = rotate(query_raw, cos_table, sin_table, False).astype(low)
    key_rot = rotate(key_raw, cos_table, sin_table, False).astype(low)
    value_low = value_raw.astype(low)
    both = jnp.concatenate([key_rot, value_low], 1)
    if paired:
        both_group = gather_pair([both], 2)[0]
    else:
        both_group = lax.all_gather(both, "shard", axis=0)
    both_group = both_group.reshape(shard_count, 2, sub_rows, 2 * kv_width)
    both_group = both_group.transpose(1, 0, 2, 3).reshape(2, seq_len, 2 * kv_width)
    allowed = (
        (own_positions[None, :, None] >= seq_positions[None, None, :])
        & (query_docs[:, :, None] == key_docs[:, None, :])
    )[:, None, None]
    query_heads = query_rot.reshape(2, sub_rows, KV_HEADS, group_ratio, HEAD_DIM)
    key_heads = both_group[:, :, :kv_width].reshape(2, seq_len, KV_HEADS, HEAD_DIM)
    value_heads = both_group[:, :, kv_width:].reshape(2, seq_len, KV_HEADS, HEAD_DIM)
    scores = (
        jnp.einsum("btkgd,bskd->bkgts", query_heads, key_heads, preferred_element_type=wide)
        * att_scale
    )
    scores = jnp.where(allowed, scores, masked_score)
    exp_scores = jnp.exp(scores - jnp.max(scores, -1, keepdims=True))
    probs = exp_scores / jnp.sum(exp_scores, -1, keepdims=True)
    probs_low = probs.astype(low)
    attn_mix = jnp.einsum("bkgts,bskd->btkgd", probs_low, value_heads, preferred_element_type=wide)
    attn_low = attn_mix.reshape(tok_count, -1).astype(low)
    branch = jnp.dot(attn_low, output_full, preferred_element_type=wide)
    middle = input_float + res_scale * branch
    normed_two = rms_norm(middle, moe_norm_gain).astype(low)
    arrived = cross(to_slots(normed_two))

    def gate_softmax(rows, chosen):
        logits = jnp.dot(rows, router_full, preferred_element_type=wide)
        top = jnp.max(jnp.where(chosen, logits, -jnp.inf), -1, keepdims=True)
        top = jnp.where(jnp.any(chosen, -1, keepdims=True), top, 0.0)
        powers = jnp.where(chosen, jnp.exp(jnp.where(chosen, logits - top, 0.0)), 0.0)
        total = jnp.sum(powers, -1, keepdims=True)
        return powers / jnp.where(total > 0.0, total, 1.0)

    gates = gate_softmax(normed_two, picks)

    gate_matrix = gate_weight[0]
    up_matrix = up_weight[0]
    down_matrix = down_weight[0]
    flat_rows = arrived.reshape(-1, model_width)
    gate_pre = jnp.dot(flat_rows, gate_matrix, preferred_element_type=wide)
    up_pre = jnp.dot(flat_rows, up_matrix, preferred_element_type=wide)
    sigmoid_gate = jax.nn.sigmoid(gate_pre)
    activated = gate_pre * sigmoid_gate
    inner = (activated * up_pre).astype(low)
    result = jnp.dot(inner, down_matrix, preferred_element_type=wide).astype(low)
    returned = cross(result.reshape(expert_axis, -1, model_width)).reshape(-1, model_width)

    flat_top = arrived_top.reshape(-1, arrived_top.shape[2])
    slot_picks = flat_top[:, model_width : model_width + expert_count] > 0.5
    slot_gates = gate_softmax(flat_rows, slot_picks)
    mine = jnp.arange(expert_count, dtype=jnp.int32)[None, :] == expert_index
    own_gate = jnp.sum(jnp.where(mine, slot_gates, 0.0), 1, keepdims=True)
    flat_grads = (own_gate * (res_scale * flat_top[:, :model_width].astype(wide))).astype(low)
    inner_grad = jnp.einsum("rd,fd->rf", flat_grads, down_matrix, preferred_element_type=wide)
    gate_pregrad = (
        inner_grad * up_pre * sigmoid_gate * (1.0 + gate_pre * (1.0 - sigmoid_gate))
    ).astype(low)
    up_pregrad = (inner_grad * activated).astype(low)
    row_grads = (
        jnp.einsum("rf,df->rd", gate_pregrad, gate_matrix, preferred_element_type=wide)
        + jnp.einsum("rf,df->rd", up_pregrad, up_matrix, preferred_element_type=wide)
    ).astype(low)
    back_grads = cross(row_grads.reshape(expert_axis, -1, model_width)).reshape(-1, model_width)
    down_wgrad = jnp.einsum("rf,rd->fd", inner, flat_grads, preferred_element_type=wide).astype(low)
    gate_wgrad = jnp.einsum(
        "rd,rf->df", flat_rows, gate_pregrad, preferred_element_type=wide
    ).astype(low)
    up_wgrad = jnp.einsum(
        "rd,rf->df", flat_rows, up_pregrad, preferred_element_type=wide
    ).astype(low)

    gates_slots = jnp.repeat(gates.T, capacity, 0) * hot.astype(wide)
    gates_high = gates_slots.astype(low)
    gates_rest = (gates_slots - gates_high.astype(wide)).astype(low)
    mixture = jnp.einsum(
        "rt,rd->td", gates_high, returned, preferred_element_type=wide
    ) + jnp.einsum("rt,rd->td", gates_rest, returned, preferred_element_type=wide)
    layer_out = (middle + res_scale * mixture).astype(low)
    grad_out = cotangent.astype(wide)
    all_dots = jnp.einsum("rd,td->rt", returned, cotangent, preferred_element_type=wide)
    grad_gates = (
        res_scale
        * jnp.sum(
            (all_dots * hot.astype(wide)).reshape(expert_count, capacity, tok_count), 1
        ).T
    )
    gate_dot = jnp.sum(gates * grad_gates, 1, keepdims=True)
    logit_grad = (gates * (grad_gates - gate_dot)).astype(low)
    router_wgrad = jnp.einsum("td,te->de", normed_two, logit_grad, preferred_element_type=wide)
    router_back = jnp.einsum("te,de->td", logit_grad, router_full, preferred_element_type=wide)
    (
        back_grads,
        layer_out,
        router_back,
        router_wgrad,
        down_wgrad,
        gate_wgrad,
        up_wgrad,
    ) = lax.optimization_barrier(
        (back_grads, layer_out, router_back, router_wgrad, down_wgrad, gate_wgrad, up_wgrad)
    )
    normed_two_grad = (
        jnp.einsum("rt,rd->td", hot, back_grads, preferred_element_type=wide) + router_back
    )
    unused_value, second_pull = jax.vjp(rms_norm, middle, moe_norm_gain)
    middle_from_norm, moe_gain_grad = second_pull(normed_two_grad)
    middle_grad = grad_out + middle_from_norm
    branch_grad = (res_scale * middle_grad).astype(low)
    output_wgrad = jnp.einsum("tq,td->qd", attn_low, branch_grad, preferred_element_type=wide)
    attn_grad = jnp.einsum(
        "td,qd->tq", branch_grad, output_full, preferred_element_type=wide
    ).astype(low)
    attn_grad = attn_grad.reshape(2, sub_rows, KV_HEADS, group_ratio, HEAD_DIM)
    prob_grad = jnp.einsum("btkgd,bskd->bkgts", attn_grad, value_heads, preferred_element_type=wide)
    value_part = jnp.einsum("bkgts,btkgd->bskd", probs_low, attn_grad, preferred_element_type=wide)
    score_grad = (probs * (prob_grad - jnp.sum(probs * prob_grad, -1, keepdims=True))).astype(low)
    query_rot_grad = att_scale * jnp.einsum(
        "bkgts,bskd->btkgd", score_grad, key_heads, preferred_element_type=wide
    )
    key_part = att_scale * jnp.einsum(
        "bkgts,btkgd->bskd", score_grad, query_heads, preferred_element_type=wide
    )
    both_part = jnp.concatenate(
        [key_part.reshape(2, seq_len, -1), value_part.reshape(2, seq_len, -1)], -1
    ).astype(low)
    both_part = both_part.reshape(2, shard_count, sub_rows, 2 * kv_width).transpose(1, 0, 2, 3)
    both_part = both_part.reshape(shard_count, tok_count, 2 * kv_width)

    def own_block(values):
        return lax.dynamic_index_in_dim(values, shard_index, 0, keepdims=False).astype(wide)

    if paired:
        both_pre = own_block(both_part) + swap_pair(both_part, 3).astype(wide)
    else:
        both_pre = lax.psum_scatter(both_part, "shard", scatter_dimension=0).astype(wide)
    query_pre_grad = rotate(
        query_rot_grad.reshape(tok_count, -1), cos_table, sin_table, True
    ).astype(low)
    key_pre_grad = rotate(both_pre[:, :kv_width], cos_table, sin_table, True).astype(low)
    value_pre_grad = both_pre[:, kv_width:].astype(low)
    both_pre_grad = jnp.concatenate([key_pre_grad, value_pre_grad], 1)
    query_wgrad = jnp.einsum("td,tq->dq", normed_one, query_pre_grad, preferred_element_type=wide)
    both_wgrad = jnp.einsum("td,tq->dq", normed_one, both_pre_grad, preferred_element_type=wide)
    normed_one_grad = (
        jnp.einsum("tq,dq->td", query_pre_grad, query_full, preferred_element_type=wide)
        + jnp.einsum("tq,dq->td", key_pre_grad, key_full, preferred_element_type=wide)
        + jnp.einsum("tq,dq->td", value_pre_grad, value_full, preferred_element_type=wide)
    )
    unused_first, first_pull = jax.vjp(rms_norm, input_float, attn_norm_gain)
    input_from_norm, attn_gain_grad = first_pull(normed_one_grad)
    input_grad = middle_grad + input_from_norm

    small = jnp.concatenate(
        [router_wgrad, attn_gain_grad[:, None], moe_gain_grad[:, None]], 1
    ).astype(low)
    small = jnp.pad(small, ((0, 0), (0, -small.shape[1] % 128)))
    batch_sums = [query_wgrad.astype(low), output_wgrad.astype(low), both_wgrad.astype(low), small]
    expert_parts = [
        a.reshape(shard_count, -1, a.shape[1]) for a in (gate_wgrad, up_wgrad, down_wgrad)
    ]
    whole_rows = model_width // shard_count
    if paired and expert_axis & (expert_axis - 1) == 0 and whole_rows % (16 * expert_axis) == 0:
        reduced = reduce_all(batch_sums, expert_parts, expert_axis, 4)
        totals = [a.astype(wide) for a in reduced[:4]]
        expert_sums = [
            own_block(own) + got.astype(wide) for own, got in zip(expert_parts, reduced[4:])
        ]
    else:
        totals = []
        for array in batch_sums:
            part = lax.psum_scatter(array, "shard", scatter_dimension=0, tiled=True)
            totals.append(lax.psum(part, "expert").astype(wide))
        expert_sums = [
            lax.psum_scatter(a, "shard", scatter_dimension=0).astype(wide) for a in expert_parts
        ]
    return (
        layer_out,
        input_grad,
        totals[3][:, expert_count],
        totals[0],
        totals[2][:, :kv_width],
        totals[2][:, kv_width:],
        totals[1],
        totals[3][:, :expert_count],
        totals[3][:, expert_count + 1],
        expert_sums[0][None],
        expert_sums[1][None],
        expert_sums[2][None],
    )


def solution(mesh):
    return jax.shard_map(
        on_device,
        mesh=mesh,
        in_specs=(
            P(("expert", "shard"), None),
            P("expert", None),
            P(("expert", "shard"), None),
            P(),
            P("shard", None),
            P("shard", None),
            P("shard", None),
            P("shard", None),
            P("shard", None),
            P(),
            P("expert", None, None),
            P("expert", None, None),
            P("expert", None, None),
            P(("expert", "shard"), None),
        ),
        out_specs=(
            P(("expert", "shard"), None),
            P(("expert", "shard"), None),
            P("shard"),
            P("shard", None),
            P("shard", None),
            P("shard", None),
            P("shard", None),
            P("shard", None),
            P("shard"),
            P("expert", "shard", None),
            P("expert", "shard", None),
            P("expert", "shard", None),
        ),
        check_vma=False,
    )
```

```python
import functools

import jax
import jax.numpy as jnp
from jax import lax
from jax.experimental import pallas as pl
from jax.experimental.pallas import tpu as pltpu
from jax.sharding import PartitionSpec as P

HEADS = 16
KV_HEADS = 8
HEAD_DIM = 64
TOP = 8


epsilon = 1e-06
res_scale = 0.22
att_scale = 0.015625
rope_base = 10000.0
masked_score = -1e30


def rms_norm(values, gain):
    return values * lax.rsqrt(jnp.mean(values * values, -1, keepdims=True) + epsilon) * gain


def doc_layout(lengths, positions):
    doc_ends = jnp.cumsum(lengths)
    past_end = positions[:, None] >= doc_ends[None, :]
    doc_index = jnp.sum(past_end.astype(jnp.int32), 1)
    doc_start = jnp.sum(jnp.where(past_end, lengths[None, :], 0), 1)
    return (doc_index, positions - doc_start)


def rope_tables(offsets):
    half_size = HEAD_DIM // 2
    frequency = rope_base ** (-2.0 * jnp.arange(half_size).astype(jnp.float32) / HEAD_DIM)
    angles = offsets.astype(jnp.float32)[:, None] * frequency[None, :]
    return (jnp.cos(angles), jnp.sin(angles))


def rotate(values, cos_table, sin_table, inverse):
    row_count = values.shape[0]
    shaped = values.reshape(row_count, -1, HEAD_DIM)
    half_size = HEAD_DIM // 2
    front_part = shaped[:, :, :half_size]
    back_part = shaped[:, :, half_size:]
    cos_wide = cos_table[:, None, :]
    sin_wide = sin_table[:, None, :]
    if inverse:
        sin_wide = -sin_wide
    turned = jnp.concatenate(
        [
            front_part * cos_wide - back_part * sin_wide,
            back_part * cos_wide + front_part * sin_wide,
        ],
        -1,
    )
    return turned.reshape(row_count, -1)


MESH_ID = pl.DeviceIdType.MESH
vmem_grant = 48 * 1024 * 1024


def greet(devices):
    barrier = pltpu.get_barrier_semaphore()
    for device in devices:
        pl.semaphore_signal(barrier, inc=1, device_id=device, device_id_type=MESH_ID)
    pl.semaphore_wait(barrier, len(devices))


def gather_kernel(count, *refs):
    sources, results = refs[:count], refs[count : 2 * count]
    send_sem, recv_sem = refs[2 * count :]
    expert_index, shard_index = lax.axis_index("expert"), lax.axis_index("shard")
    other = (expert_index, 1 - shard_index)
    greet([other])
    copies = []
    for at in range(count):
        copy = pltpu.make_async_remote_copy(
            src_ref=sources[at],
            dst_ref=results[at].at[shard_index],
            send_sem=send_sem.at[at],
            recv_sem=recv_sem.at[at],
            device_id=other,
            device_id_type=MESH_ID,
        )
        copy.start()
        copies.append(copy)
    for at in range(count):
        step = 32

        def one(index, carry, at=at, step=step):
            rows = pl.ds(pl.multiple_of(index * step, step), step)
            results[at][shard_index, rows, :] = sources[at][rows, :]
            return carry

        lax.fori_loop(0, sources[at].shape[0] // step, one, 0)
    for copy in copies:
        copy.wait()


def gather_pair(arrays, identity):
    count = len(arrays)
    spec = pl.BlockSpec(memory_space=pltpu.VMEM)
    return pl.pallas_call(
        functools.partial(gather_kernel, count),
        out_shape=[jax.ShapeDtypeStruct((2,) + a.shape, a.dtype) for a in arrays],
        in_specs=[spec] * count,
        out_specs=[spec] * count,
        scratch_shapes=[pltpu.SemaphoreType.DMA((count,))] * 2,
        compiler_params=pltpu.CompilerParams(
            collective_id=identity, has_side_effects=True, vmem_limit_bytes=vmem_grant
        ),
    )(*arrays)


def swap_kernel(source, result, send_sem, recv_sem):
    expert_index, shard_index = lax.axis_index("expert"), lax.axis_index("shard")
    other = (expert_index, 1 - shard_index)
    greet([other])
    copy = pltpu.make_async_remote_copy(
        src_ref=source.at[1 - shard_index],
        dst_ref=result,
        send_sem=send_sem,
        recv_sem=recv_sem,
        device_id=other,
        device_id_type=MESH_ID,
    )
    copy.start()
    copy.wait()


def swap_pair(array, identity):
    return pl.pallas_call(
        swap_kernel,
        out_shape=jax.ShapeDtypeStruct(array.shape[1:], array.dtype),
        in_specs=[pl.BlockSpec(memory_space=pl.ANY)],
        out_specs=pl.BlockSpec(memory_space=pl.ANY),
        scratch_shapes=[pltpu.SemaphoreType.DMA, pltpu.SemaphoreType.DMA],
        compiler_params=pltpu.CompilerParams(collective_id=identity, has_side_effects=True),
    )(array)


def add_rows(target, target_at, first, first_at, second, second_at, rows, columns):
    step = min(rows, 32)

    def one(index, carry):
        row = index * step
        into = pl.ds(pl.multiple_of(target_at + row, step), step)
        left = pl.ds(pl.multiple_of(first_at + row, step), step)
        right = pl.ds(pl.multiple_of(second_at + row, step), step)
        total = first[left, columns].astype(jnp.float32) + second[right, columns].astype(
            jnp.float32
        )
        target[into, columns] = total.astype(target.dtype)
        return carry

    lax.fori_loop(0, rows // step, one, 0)


def bit_order(array, levels):
    if levels < 3:
        return list(range(levels))
    first = [[0, 1, 2], [1, 2, 0], [2, 0, 1]][array % 3]
    return first + list(range(3, levels))


def reduce_kernel(levels, parts, swaps, *refs):
    refs = list(refs)

    def take(amount):
        taken = refs[:amount]
        del refs[:amount]
        return taken

    sources, swap_sources = take(parts), take(swaps)
    totals, swap_results = take(parts), take(swaps)
    near, far, partial = take(parts), take(parts), take(parts)
    send_sem, recv_sem, swap_send, swap_recv = refs
    expert_index, shard_index = lax.axis_index("expert"), lax.axis_index("shard")
    other = (expert_index, 1 - shard_index)
    held = [(expert_index // (1 << bit)) % 2 for bit in range(levels)]
    partners = [
        (expert_index + (1 << bit) * (1 - 2 * held[bit]), shard_index) for bit in range(levels)
    ]
    greet([other] + partners)
    rows = totals[0].shape[0]
    lanes = []
    for piece in range(2):
        for array in range(parts):
            width = totals[array].shape[1]
            if width % 256 == 0:
                columns = pl.ds(piece * (width // 2), width // 2)
            elif piece == 0:
                columns = pl.ds(0, width)
            else:
                continue
            lanes.append((array, columns, bit_order(array, levels)))

    def send(lane, step, source, source_rows, target, target_rows, device):
        columns = lanes[lane][1]
        copy = pltpu.make_async_remote_copy(
            src_ref=source.at[source_rows, columns],
            dst_ref=target.at[target_rows, columns],
            send_sem=send_sem.at[lane, step],
            recv_sem=recv_sem.at[lane, step],
            device_id=device,
            device_id_type=MESH_ID,
        )
        copy.start()
        return copy

    flying = []
    away = pl.ds(pl.multiple_of((1 - shard_index) * rows, rows), rows)
    for lane, (array, columns, order) in enumerate(lanes):
        flying.append(send(lane, 0, sources[array], away, near[array], pl.ds(0, rows), other))
    swapping = []
    for at in range(swaps):
        copy = pltpu.make_async_remote_copy(
            src_ref=swap_sources[at].at[1 - shard_index],
            dst_ref=swap_results[at],
            send_sem=swap_send.at[at],
            recv_sem=swap_recv.at[at],
            device_id=other,
            device_id_type=MESH_ID,
        )
        copy.start()
        swapping.append(copy)
    starts = [0] * len(lanes)
    size = rows
    landing = 0
    for step in range(2 * levels + 1):
        kept = size // 2 if 1 <= step <= levels else size
        for lane, (array, columns, order) in enumerate(lanes):
            flying[lane].wait()
            if step == 0:
                add_rows(
                    partial[array],
                    0,
                    sources[array],
                    shard_index * rows,
                    near[array],
                    0,
                    rows,
                    columns,
                )
            elif step <= levels:
                starts[lane] = starts[lane] + held[order[step - 1]] * kept
                add_rows(
                    totals[array] if step == levels else partial[array],
                    starts[lane],
                    partial[array],
                    starts[lane],
                    far[array],
                    landing,
                    kept,
                    columns,
                )
            else:
                starts[lane] = starts[lane] - held[order[2 * levels - step]] * size
            if step < levels:
                half = kept // 2
                bit = order[step]
                leaving = pl.multiple_of(starts[lane] + (1 - held[bit]) * half, half)
                room = 0 if step == 0 else landing + kept
                flying[lane] = send(
                    lane,
                    step + 1,
                    partial[array],
                    pl.ds(leaving, half),
                    far[array],
                    pl.ds(room, half),
                    partners[bit],
                )
            elif step < 2 * levels:
                whole = kept if step == levels else size * 2
                region = pl.ds(pl.multiple_of(starts[lane], whole), whole)
                bit = order[2 * levels - 1 - step]
                flying[lane] = send(
                    lane, step + 1, totals[array], region, totals[array], region, partners[bit]
                )
        if 1 <= step <= levels:
            landing += kept
            size = kept
        elif step > levels:
            size *= 2
    for copy in swapping:
        copy.wait()


def reduce_all(sources, swap_sources, expert_count, identity):
    parts, swaps = len(sources), len(swap_sources)
    levels = expert_count.bit_length() - 1
    rows = sources[0].shape[0] // 2
    spec = pl.BlockSpec(memory_space=pltpu.VMEM)
    return pl.pallas_call(
        functools.partial(reduce_kernel, levels, parts, swaps),
        out_shape=[jax.ShapeDtypeStruct((rows, a.shape[1]), a.dtype) for a in sources]
        + [jax.ShapeDtypeStruct(a.shape[1:], a.dtype) for a in swap_sources],
        in_specs=[spec] * (parts + swaps),
        out_specs=[spec] * (parts + swaps),
        scratch_shapes=[pltpu.VMEM((rows, a.shape[1]), a.dtype) for a in list(sources) * 3]
        + [pltpu.SemaphoreType.DMA((2 * parts, 2 * levels + 1))] * 2
        + [pltpu.SemaphoreType.DMA((swaps,))] * 2,
        compiler_params=pltpu.CompilerParams(
            collective_id=identity, has_side_effects=True, vmem_limit_bytes=vmem_grant
        ),
    )(*sources, *swap_sources)


def on_device(
    hidden_in,
    doc_lengths,
    routes,
    attn_norm_gain,
    query_weight,
    key_weight,
    value_weight,
    output_weight,
    router_weight,
    moe_norm_gain,
    gate_weight,
    up_weight,
    down_weight,
    cotangent,
):
    low = jnp.bfloat16
    wide = jnp.float32
    tok_count, model_width = hidden_in.shape
    shard_index = lax.axis_index("shard")
    shard_count = lax.axis_size("shard")
    expert_axis = lax.axis_size("expert")
    expert_index = lax.axis_index("expert")
    paired = shard_count == 2
    expert_count = router_weight.shape[1]
    capacity = 17 * tok_count * TOP // (16 * expert_count)
    capacity = -(-capacity // 8) * 8
    sub_rows = tok_count // 2
    seq_len = sub_rows * shard_count
    group_ratio = HEADS // KV_HEADS
    kv_width = key_weight.shape[1]

    picks = jnp.any(
        routes[:, :, None] == jnp.arange(expert_count, dtype=jnp.int32)[None, None, :], 1
    )
    picks_low = picks.astype(low)
    earlier = jnp.tril(jnp.ones((tok_count, tok_count), low), -1)
    place = jnp.dot(earlier, picks_low, preferred_element_type=wide).astype(jnp.int32)
    place = jnp.where(picks, place, -1)
    hot = (
        place.T[:, None, :] == jnp.arange(capacity, dtype=jnp.int32)[None, :, None]
    ).astype(low)
    hot = hot.reshape(expert_count * capacity, tok_count)

    def to_slots(values):
        rows = jnp.dot(hot, values, preferred_element_type=wide).astype(low)
        return rows.reshape(expert_count, capacity, -1)

    def cross(values):
        return lax.all_to_all(values, "expert", split_axis=0, concat_axis=0, tiled=True)

    picks_wide = jnp.pad(picks_low, ((0, 0), (0, -expert_count % 128)))
    arrived_top = cross(to_slots(jnp.concatenate([cotangent, picks_wide], 1)))

    router_wide = jnp.pad(router_weight, ((0, 0), (0, -expert_count % 128)))
    weights = [query_weight, key_weight, value_weight, output_weight, router_wide]
    if paired:
        gathered = [a.reshape(-1, a.shape[2]) for a in gather_pair(weights, 1)]
    else:
        gathered = [lax.all_gather(a, "shard", axis=0, tiled=True) for a in weights]
    query_full, key_full, value_full, output_full, router_padded = gathered
    router_full = router_padded[:, :expert_count]

    input_float = hidden_in.astype(wide)
    normed_one = rms_norm(input_float, attn_norm_gain).astype(low)
    query_raw = jnp.dot(normed_one, query_full, preferred_element_type=wide)
    key_raw = jnp.dot(normed_one, key_full, preferred_element_type=wide)
    value_raw = jnp.dot(normed_one, value_full, preferred_element_type=wide)
    own_positions = shard_index * sub_rows + jnp.arange(sub_rows, dtype=jnp.int32)
    seq_positions = jnp.arange(seq_len, dtype=jnp.int32)
    layout_both = jax.vmap(doc_layout, in_axes=(0, None))
    query_docs, query_offsets = layout_both(doc_lengths, own_positions)
    key_docs, unused_offsets = layout_both(doc_lengths, seq_positions)
    cos_table, sin_table = rope_tables(query_offsets.reshape(-1))
    query_rot = rotate(query_raw, cos_table, sin_table, False).astype(low)
    key_rot = rotate(key_raw, cos_table, sin_table, False).astype(low)
    value_low = value_raw.astype(low)
    both = jnp.concatenate([key_rot, value_low], 1)
    if paired:
        both_group = gather_pair([both], 2)[0]
    else:
        both_group = lax.all_gather(both, "shard", axis=0)
    both_group = both_group.reshape(shard_count, 2, sub_rows, 2 * kv_width)
    both_group = both_group.transpose(1, 0, 2, 3).reshape(2, seq_len, 2 * kv_width)
    allowed = (
        (own_positions[None, :, None] >= seq_positions[None, None, :])
        & (query_docs[:, :, None] == key_docs[:, None, :])
    )[:, None, None]
    query_heads = query_rot.reshape(2, sub_rows, KV_HEADS, group_ratio, HEAD_DIM)
    key_heads = both_group[:, :, :kv_width].reshape(2, seq_len, KV_HEADS, HEAD_DIM)
    value_heads = both_group[:, :, kv_width:].reshape(2, seq_len, KV_HEADS, HEAD_DIM)
    scores = (
        jnp.einsum("btkgd,bskd->bkgts", query_heads, key_heads, preferred_element_type=wide)
        * att_scale
    )
    scores = jnp.where(allowed, scores, masked_score)
    exp_scores = jnp.exp(scores - jnp.max(scores, -1, keepdims=True))
    probs = exp_scores / jnp.sum(exp_scores, -1, keepdims=True)
    probs_low = probs.astype(low)
    attn_mix = jnp.einsum("bkgts,bskd->btkgd", probs_low, value_heads, preferred_element_type=wide)
    attn_low = attn_mix.reshape(tok_count, -1).astype(low)
    branch = jnp.dot(attn_low, output_full, preferred_element_type=wide)
    middle = input_float + res_scale * branch
    normed_two = rms_norm(middle, moe_norm_gain).astype(low)
    send_rows, arrived_top = lax.optimization_barrier((to_slots(normed_two), arrived_top))
    arrived = cross(send_rows)

    def gate_softmax(rows, chosen):
        logits = jnp.dot(rows, router_full, preferred_element_type=wide)
        top = jnp.max(jnp.where(chosen, logits, -jnp.inf), -1, keepdims=True)
        top = jnp.where(jnp.any(chosen, -1, keepdims=True), top, 0.0)
        powers = jnp.where(chosen, jnp.exp(jnp.where(chosen, logits - top, 0.0)), 0.0)
        total = jnp.sum(powers, -1, keepdims=True)
        return powers / jnp.where(total > 0.0, total, 1.0)

    gates = gate_softmax(normed_two, picks)

    gate_matrix = gate_weight[0]
    up_matrix = up_weight[0]
    down_matrix = down_weight[0]
    flat_rows = arrived.reshape(-1, model_width)
    gate_pre = jnp.dot(flat_rows, gate_matrix, preferred_element_type=wide)
    up_pre = jnp.dot(flat_rows, up_matrix, preferred_element_type=wide)
    sigmoid_gate = jax.nn.sigmoid(gate_pre)
    activated = gate_pre * sigmoid_gate
    inner = (activated * up_pre).astype(low)
    result = jnp.dot(inner, down_matrix, preferred_element_type=wide).astype(low)
    returned = cross(result.reshape(expert_axis, -1, model_width)).reshape(-1, model_width)

    flat_top = arrived_top.reshape(-1, arrived_top.shape[2])
    slot_picks = flat_top[:, model_width : model_width + expert_count] > 0.5
    slot_gates = gate_softmax(flat_rows, slot_picks)
    mine = jnp.arange(expert_count, dtype=jnp.int32)[None, :] == expert_index
    own_gate = jnp.sum(jnp.where(mine, slot_gates, 0.0), 1, keepdims=True)
    flat_grads = (own_gate * (res_scale * flat_top[:, :model_width].astype(wide))).astype(low)
    inner_grad = jnp.einsum("rd,fd->rf", flat_grads, down_matrix, preferred_element_type=wide)
    gate_pregrad = (
        inner_grad * up_pre * sigmoid_gate * (1.0 + gate_pre * (1.0 - sigmoid_gate))
    ).astype(low)
    up_pregrad = (inner_grad * activated).astype(low)
    row_grads = (
        jnp.einsum("rf,df->rd", gate_pregrad, gate_matrix, preferred_element_type=wide)
        + jnp.einsum("rf,df->rd", up_pregrad, up_matrix, preferred_element_type=wide)
    ).astype(low)
    back_grads = cross(row_grads.reshape(expert_axis, -1, model_width)).reshape(-1, model_width)
    down_wgrad = jnp.einsum("rf,rd->fd", inner, flat_grads, preferred_element_type=wide).astype(low)
    gate_wgrad = jnp.einsum(
        "rd,rf->df", flat_rows, gate_pregrad, preferred_element_type=wide
    ).astype(low)
    up_wgrad = jnp.einsum(
        "rd,rf->df", flat_rows, up_pregrad, preferred_element_type=wide
    ).astype(low)

    gates_slots = jnp.repeat(gates.T, capacity, 0) * hot.astype(wide)
    gates_high = gates_slots.astype(low)
    gates_rest = (gates_slots - gates_high.astype(wide)).astype(low)
    mixture = jnp.einsum(
        "rt,rd->td", gates_high, returned, preferred_element_type=wide
    ) + jnp.einsum("rt,rd->td", gates_rest, returned, preferred_element_type=wide)
    layer_out = (middle + res_scale * mixture).astype(low)
    grad_out = cotangent.astype(wide)
    all_dots = jnp.einsum("rd,td->rt", returned, cotangent, preferred_element_type=wide)
    grad_gates = (
        res_scale
        * jnp.sum(
            (all_dots * hot.astype(wide)).reshape(expert_count, capacity, tok_count), 1
        ).T
    )
    gate_dot = jnp.sum(gates * grad_gates, 1, keepdims=True)
    logit_grad = (gates * (grad_gates - gate_dot)).astype(low)
    router_wgrad = jnp.einsum("td,te->de", normed_two, logit_grad, preferred_element_type=wide)
    router_back = jnp.einsum("te,de->td", logit_grad, router_full, preferred_element_type=wide)
    (
        back_grads,
        layer_out,
        router_back,
        router_wgrad,
        down_wgrad,
        gate_wgrad,
        up_wgrad,
    ) = lax.optimization_barrier(
        (back_grads, layer_out, router_back, router_wgrad, down_wgrad, gate_wgrad, up_wgrad)
    )
    normed_two_grad = (
        jnp.einsum("rt,rd->td", hot, back_grads, preferred_element_type=wide) + router_back
    )
    unused_value, second_pull = jax.vjp(rms_norm, middle, moe_norm_gain)
    middle_from_norm, moe_gain_grad = second_pull(normed_two_grad)
    middle_grad = grad_out + middle_from_norm
    branch_grad = (res_scale * middle_grad).astype(low)
    output_wgrad = jnp.einsum("tq,td->qd", attn_low, branch_grad, preferred_element_type=wide)
    attn_grad = jnp.einsum(
        "td,qd->tq", branch_grad, output_full, preferred_element_type=wide
    ).astype(low)
    attn_grad = attn_grad.reshape(2, sub_rows, KV_HEADS, group_ratio, HEAD_DIM)
    prob_grad = jnp.einsum("btkgd,bskd->bkgts", attn_grad, value_heads, preferred_element_type=wide)
    value_part = jnp.einsum("bkgts,btkgd->bskd", probs_low, attn_grad, preferred_element_type=wide)
    score_grad = (probs * (prob_grad - jnp.sum(probs * prob_grad, -1, keepdims=True))).astype(low)
    query_rot_grad = att_scale * jnp.einsum(
        "bkgts,bskd->btkgd", score_grad, key_heads, preferred_element_type=wide
    )
    key_part = att_scale * jnp.einsum(
        "bkgts,btkgd->bskd", score_grad, query_heads, preferred_element_type=wide
    )
    both_part = jnp.concatenate(
        [key_part.reshape(2, seq_len, -1), value_part.reshape(2, seq_len, -1)], -1
    ).astype(low)
    both_part = both_part.reshape(2, shard_count, sub_rows, 2 * kv_width).transpose(1, 0, 2, 3)
    both_part = both_part.reshape(shard_count, tok_count, 2 * kv_width)

    def own_block(values):
        return lax.dynamic_index_in_dim(values, shard_index, 0, keepdims=False).astype(wide)

    if paired:
        both_pre = own_block(both_part) + swap_pair(both_part, 3).astype(wide)
    else:
        both_pre = lax.psum_scatter(both_part, "shard", scatter_dimension=0).astype(wide)
    query_pre_grad = rotate(
        query_rot_grad.reshape(tok_count, -1), cos_table, sin_table, True
    ).astype(low)
    key_pre_grad = rotate(both_pre[:, :kv_width], cos_table, sin_table, True).astype(low)
    value_pre_grad = both_pre[:, kv_width:].astype(low)
    both_pre_grad = jnp.concatenate([key_pre_grad, value_pre_grad], 1)
    query_wgrad = jnp.einsum("td,tq->dq", normed_one, query_pre_grad, preferred_element_type=wide)
    both_wgrad = jnp.einsum("td,tq->dq", normed_one, both_pre_grad, preferred_element_type=wide)
    normed_one_grad = (
        jnp.einsum("tq,dq->td", query_pre_grad, query_full, preferred_element_type=wide)
        + jnp.einsum("tq,dq->td", key_pre_grad, key_full, preferred_element_type=wide)
        + jnp.einsum("tq,dq->td", value_pre_grad, value_full, preferred_element_type=wide)
    )
    unused_first, first_pull = jax.vjp(rms_norm, input_float, attn_norm_gain)
    input_from_norm, attn_gain_grad = first_pull(normed_one_grad)
    input_grad = middle_grad + input_from_norm

    small = jnp.concatenate(
        [router_wgrad, attn_gain_grad[:, None], moe_gain_grad[:, None]], 1
    ).astype(low)
    small = jnp.pad(small, ((0, 0), (0, -small.shape[1] % 128)))
    batch_sums = [query_wgrad.astype(low), output_wgrad.astype(low), both_wgrad.astype(low), small]
    expert_parts = [
        a.reshape(shard_count, -1, a.shape[1]) for a in (gate_wgrad, up_wgrad, down_wgrad)
    ]
    whole_rows = model_width // shard_count
    if paired and expert_axis & (expert_axis - 1) == 0 and whole_rows % (16 * expert_axis) == 0:
        reduced = reduce_all(batch_sums, expert_parts, expert_axis, 4)
        totals = [a.astype(wide) for a in reduced[:4]]
        expert_sums = [
            own_block(own) + got.astype(wide) for own, got in zip(expert_parts, reduced[4:])
        ]
    else:
        totals = []
        for array in batch_sums:
            part = lax.psum_scatter(array, "shard", scatter_dimension=0, tiled=True)
            totals.append(lax.psum(part, "expert").astype(wide))
        expert_sums = [
            lax.psum_scatter(a, "shard", scatter_dimension=0).astype(wide) for a in expert_parts
        ]
    return (
        layer_out,
        input_grad,
        totals[3][:, expert_count],
        totals[0],
        totals[2][:, :kv_width],
        totals[2][:, kv_width:],
        totals[1],
        totals[3][:, :expert_count],
        totals[3][:, expert_count + 1],
        expert_sums[0][None],
        expert_sums[1][None],
        expert_sums[2][None],
    )


def solution(mesh):
    return jax.shard_map(
        on_device,
        mesh=mesh,
        in_specs=(
            P(("expert", "shard"), None),
            P("expert", None),
            P(("expert", "shard"), None),
            P(),
            P("shard", None),
            P("shard", None),
            P("shard", None),
            P("shard", None),
            P("shard", None),
            P(),
            P("expert", None, None),
            P("expert", None, None),
            P("expert", None, None),
            P(("expert", "shard"), None),
        ),
        out_specs=(
            P(("expert", "shard"), None),
            P(("expert", "shard"), None),
            P("shard"),
            P("shard", None),
            P("shard", None),
            P("shard", None),
            P("shard", None),
            P("shard", None),
            P("shard"),
            P("expert", "shard", None),
            P("expert", "shard", None),
            P("expert", "shard", None),
        ),
        check_vma=False,
    )
```

```python
import functools

import jax
import jax.numpy as jnp
from jax import lax
from jax.experimental import pallas as pl
from jax.experimental.pallas import tpu as pltpu
from jax.sharding import PartitionSpec as P

HEADS = 16
KV_HEADS = 8
HEAD_DIM = 64
TOP = 8


epsilon = 1e-06
res_scale = 0.22
att_scale = 0.015625
rope_base = 10000.0
masked_score = -1e30


def rms_norm(values, gain):
    return values * lax.rsqrt(jnp.mean(values * values, -1, keepdims=True) + epsilon) * gain


def doc_layout(lengths, positions):
    doc_ends = jnp.cumsum(lengths)
    past_end = positions[:, None] >= doc_ends[None, :]
    doc_index = jnp.sum(past_end.astype(jnp.int32), 1)
    doc_start = jnp.sum(jnp.where(past_end, lengths[None, :], 0), 1)
    return (doc_index, positions - doc_start)


def rope_tables(offsets):
    half_size = HEAD_DIM // 2
    frequency = rope_base ** (-2.0 * jnp.arange(half_size).astype(jnp.float32) / HEAD_DIM)
    angles = offsets.astype(jnp.float32)[:, None] * frequency[None, :]
    return (jnp.cos(angles), jnp.sin(angles))


def rotate(values, cos_table, sin_table, inverse):
    row_count = values.shape[0]
    shaped = values.reshape(row_count, -1, HEAD_DIM)
    half_size = HEAD_DIM // 2
    front_part = shaped[:, :, :half_size]
    back_part = shaped[:, :, half_size:]
    cos_wide = cos_table[:, None, :]
    sin_wide = sin_table[:, None, :]
    if inverse:
        sin_wide = -sin_wide
    turned = jnp.concatenate(
        [
            front_part * cos_wide - back_part * sin_wide,
            back_part * cos_wide + front_part * sin_wide,
        ],
        -1,
    )
    return turned.reshape(row_count, -1)


MESH_ID = pl.DeviceIdType.MESH
vmem_grant = 48 * 1024 * 1024


def greet(devices):
    barrier = pltpu.get_barrier_semaphore()
    for device in devices:
        pl.semaphore_signal(barrier, inc=1, device_id=device, device_id_type=MESH_ID)
    pl.semaphore_wait(barrier, len(devices))


def gather_kernel(count, *refs):
    sources, results = refs[:count], refs[count : 2 * count]
    send_sem, recv_sem = refs[2 * count :]
    expert_index, shard_index = lax.axis_index("expert"), lax.axis_index("shard")
    other = (expert_index, 1 - shard_index)
    greet([other])
    copies = []
    for at in range(count):
        copy = pltpu.make_async_remote_copy(
            src_ref=sources[at],
            dst_ref=results[at].at[shard_index],
            send_sem=send_sem.at[at],
            recv_sem=recv_sem.at[at],
            device_id=other,
            device_id_type=MESH_ID,
        )
        copy.start()
        copies.append(copy)
    for at in range(count):
        step = 32

        def one(index, carry, at=at, step=step):
            rows = pl.ds(pl.multiple_of(index * step, step), step)
            results[at][shard_index, rows, :] = sources[at][rows, :]
            return carry

        lax.fori_loop(0, sources[at].shape[0] // step, one, 0)
    for copy in copies:
        copy.wait()


def gather_pair(arrays, identity):
    count = len(arrays)
    spec = pl.BlockSpec(memory_space=pltpu.VMEM)
    return pl.pallas_call(
        functools.partial(gather_kernel, count),
        out_shape=[jax.ShapeDtypeStruct((2,) + a.shape, a.dtype) for a in arrays],
        in_specs=[spec] * count,
        out_specs=[spec] * count,
        scratch_shapes=[pltpu.SemaphoreType.DMA((count,))] * 2,
        compiler_params=pltpu.CompilerParams(
            collective_id=identity, has_side_effects=True, vmem_limit_bytes=vmem_grant
        ),
    )(*arrays)


def swap_kernel(source, result, send_sem, recv_sem):
    expert_index, shard_index = lax.axis_index("expert"), lax.axis_index("shard")
    other = (expert_index, 1 - shard_index)
    greet([other])
    copy = pltpu.make_async_remote_copy(
        src_ref=source.at[1 - shard_index],
        dst_ref=result,
        send_sem=send_sem,
        recv_sem=recv_sem,
        device_id=other,
        device_id_type=MESH_ID,
    )
    copy.start()
    copy.wait()


def swap_pair(array, identity):
    return pl.pallas_call(
        swap_kernel,
        out_shape=jax.ShapeDtypeStruct(array.shape[1:], array.dtype),
        in_specs=[pl.BlockSpec(memory_space=pl.ANY)],
        out_specs=pl.BlockSpec(memory_space=pl.ANY),
        scratch_shapes=[pltpu.SemaphoreType.DMA, pltpu.SemaphoreType.DMA],
        compiler_params=pltpu.CompilerParams(collective_id=identity, has_side_effects=True),
    )(array)


def add_rows(target, target_at, first, first_at, second, second_at, rows, columns):
    step = min(rows, 32)

    def one(index, carry):
        row = index * step
        into = pl.ds(pl.multiple_of(target_at + row, step), step)
        left = pl.ds(pl.multiple_of(first_at + row, step), step)
        right = pl.ds(pl.multiple_of(second_at + row, step), step)
        total = first[left, columns].astype(jnp.float32) + second[right, columns].astype(
            jnp.float32
        )
        target[into, columns] = total.astype(target.dtype)
        return carry

    lax.fori_loop(0, rows // step, one, 0)


def bit_order(array, levels):
    if levels < 3:
        return list(range(levels))
    first = [[0, 1, 2], [1, 2, 0], [2, 0, 1]][array % 3]
    return first + list(range(3, levels))


def reduce_kernel(levels, parts, swaps, *refs):
    refs = list(refs)

    def take(amount):
        taken = refs[:amount]
        del refs[:amount]
        return taken

    sources, swap_sources = take(parts), take(swaps)
    totals, swap_results = take(parts), take(swaps)
    near, far, partial = take(parts), take(parts), take(parts)
    send_sem, recv_sem, swap_send, swap_recv = refs
    expert_index, shard_index = lax.axis_index("expert"), lax.axis_index("shard")
    other = (expert_index, 1 - shard_index)
    held = [(expert_index // (1 << bit)) % 2 for bit in range(levels)]
    partners = [
        (expert_index + (1 << bit) * (1 - 2 * held[bit]), shard_index) for bit in range(levels)
    ]
    greet([other] + partners)
    rows = totals[0].shape[0]
    lanes = []
    for piece in range(2):
        for array in range(parts):
            width = totals[array].shape[1]
            if width % 256 == 0:
                columns = pl.ds(piece * (width // 2), width // 2)
            elif piece == 0:
                columns = pl.ds(0, width)
            else:
                continue
            lanes.append((array, columns, bit_order(array, levels)))

    def send(lane, step, source, source_rows, target, target_rows, device):
        columns = lanes[lane][1]
        copy = pltpu.make_async_remote_copy(
            src_ref=source.at[source_rows, columns],
            dst_ref=target.at[target_rows, columns],
            send_sem=send_sem.at[lane, step],
            recv_sem=recv_sem.at[lane, step],
            device_id=device,
            device_id_type=MESH_ID,
        )
        copy.start()
        return copy

    flying = []
    away = pl.ds(pl.multiple_of((1 - shard_index) * rows, rows), rows)
    for lane, (array, columns, order) in enumerate(lanes):
        flying.append(send(lane, 0, sources[array], away, near[array], pl.ds(0, rows), other))
    swapping = []
    for at in range(swaps):
        copy = pltpu.make_async_remote_copy(
            src_ref=swap_sources[at].at[1 - shard_index],
            dst_ref=swap_results[at],
            send_sem=swap_send.at[at],
            recv_sem=swap_recv.at[at],
            device_id=other,
            device_id_type=MESH_ID,
        )
        copy.start()
        swapping.append(copy)
    starts = [0] * len(lanes)
    size = rows
    landing = 0
    for step in range(2 * levels + 1):
        kept = size // 2 if 1 <= step <= levels else size
        for lane, (array, columns, order) in enumerate(lanes):
            flying[lane].wait()
            if step == 0:
                add_rows(
                    partial[array],
                    0,
                    sources[array],
                    shard_index * rows,
                    near[array],
                    0,
                    rows,
                    columns,
                )
            elif step <= levels:
                starts[lane] = starts[lane] + held[order[step - 1]] * kept
                add_rows(
                    totals[array] if step == levels else partial[array],
                    starts[lane],
                    partial[array],
                    starts[lane],
                    far[array],
                    landing,
                    kept,
                    columns,
                )
            else:
                starts[lane] = starts[lane] - held[order[2 * levels - step]] * size
            if step < levels:
                half = kept // 2
                bit = order[step]
                leaving = pl.multiple_of(starts[lane] + (1 - held[bit]) * half, half)
                room = 0 if step == 0 else landing + kept
                flying[lane] = send(
                    lane,
                    step + 1,
                    partial[array],
                    pl.ds(leaving, half),
                    far[array],
                    pl.ds(room, half),
                    partners[bit],
                )
            elif step < 2 * levels:
                whole = kept if step == levels else size * 2
                region = pl.ds(pl.multiple_of(starts[lane], whole), whole)
                bit = order[2 * levels - 1 - step]
                flying[lane] = send(
                    lane, step + 1, totals[array], region, totals[array], region, partners[bit]
                )
        if 1 <= step <= levels:
            landing += kept
            size = kept
        elif step > levels:
            size *= 2
    for copy in swapping:
        copy.wait()


def reduce_all(sources, swap_sources, expert_count, identity):
    parts, swaps = len(sources), len(swap_sources)
    levels = expert_count.bit_length() - 1
    rows = sources[0].shape[0] // 2
    spec = pl.BlockSpec(memory_space=pltpu.VMEM)
    return pl.pallas_call(
        functools.partial(reduce_kernel, levels, parts, swaps),
        out_shape=[jax.ShapeDtypeStruct((rows, a.shape[1]), a.dtype) for a in sources]
        + [jax.ShapeDtypeStruct(a.shape[1:], a.dtype) for a in swap_sources],
        in_specs=[spec] * (parts + swaps),
        out_specs=[spec] * (parts + swaps),
        scratch_shapes=[pltpu.VMEM((rows, a.shape[1]), a.dtype) for a in list(sources) * 3]
        + [pltpu.SemaphoreType.DMA((2 * parts, 2 * levels + 1))] * 2
        + [pltpu.SemaphoreType.DMA((swaps,))] * 2,
        compiler_params=pltpu.CompilerParams(
            collective_id=identity, has_side_effects=True, vmem_limit_bytes=vmem_grant
        ),
    )(*sources, *swap_sources)


def on_device(
    hidden_in,
    doc_lengths,
    routes,
    attn_norm_gain,
    query_weight,
    key_weight,
    value_weight,
    output_weight,
    router_weight,
    moe_norm_gain,
    gate_weight,
    up_weight,
    down_weight,
    cotangent,
):
    low = jnp.bfloat16
    wide = jnp.float32
    tok_count, model_width = hidden_in.shape
    shard_index = lax.axis_index("shard")
    shard_count = lax.axis_size("shard")
    expert_axis = lax.axis_size("expert")
    expert_index = lax.axis_index("expert")
    paired = shard_count == 2
    expert_count = router_weight.shape[1]
    capacity = 17 * tok_count * TOP // (16 * expert_count)
    capacity = -(-capacity // 8) * 8
    sub_rows = tok_count // 2
    seq_len = sub_rows * shard_count
    group_ratio = HEADS // KV_HEADS
    kv_width = key_weight.shape[1]

    picks = jnp.any(
        routes[:, :, None] == jnp.arange(expert_count, dtype=jnp.int32)[None, None, :], 1
    )
    picks_low = picks.astype(low)
    earlier = jnp.tril(jnp.ones((tok_count, tok_count), low), -1)
    place = jnp.dot(earlier, picks_low, preferred_element_type=wide).astype(jnp.int32)
    place = jnp.where(picks, place, -1)
    hot = (
        place.T[:, None, :] == jnp.arange(capacity, dtype=jnp.int32)[None, :, None]
    ).astype(low)
    hot = hot.reshape(expert_count * capacity, tok_count)

    def to_slots(values):
        rows = jnp.dot(hot, values, preferred_element_type=wide).astype(low)
        return rows.reshape(expert_count, capacity, -1)

    def cross(values):
        return lax.all_to_all(values, "expert", split_axis=0, concat_axis=0, tiled=True)

    picks_wide = jnp.pad(picks_low, ((0, 0), (0, -expert_count % 128)))
    arrived_top = cross(to_slots(jnp.concatenate([cotangent, picks_wide], 1)))

    router_wide = jnp.pad(router_weight, ((0, 0), (0, -expert_count % 128)))
    weights = [query_weight, key_weight, value_weight, output_weight, router_wide]
    if paired:
        gathered = [a.reshape(-1, a.shape[2]) for a in gather_pair(weights, 1)]
    else:
        gathered = [lax.all_gather(a, "shard", axis=0, tiled=True) for a in weights]
    query_full, key_full, value_full, output_full, router_padded = gathered
    router_full = router_padded[:, :expert_count]

    input_float = hidden_in.astype(wide)
    normed_one = rms_norm(input_float, attn_norm_gain).astype(low)
    query_raw = jnp.dot(normed_one, query_full, preferred_element_type=wide)
    key_raw = jnp.dot(normed_one, key_full, preferred_element_type=wide)
    value_raw = jnp.dot(normed_one, value_full, preferred_element_type=wide)
    own_positions = shard_index * sub_rows + jnp.arange(sub_rows, dtype=jnp.int32)
    seq_positions = jnp.arange(seq_len, dtype=jnp.int32)
    layout_both = jax.vmap(doc_layout, in_axes=(0, None))
    query_docs, query_offsets = layout_both(doc_lengths, own_positions)
    key_docs, unused_offsets = layout_both(doc_lengths, seq_positions)
    cos_table, sin_table = rope_tables(query_offsets.reshape(-1))
    query_rot = rotate(query_raw, cos_table, sin_table, False).astype(low)
    key_rot = rotate(key_raw, cos_table, sin_table, False).astype(low)
    value_low = value_raw.astype(low)
    both = jnp.concatenate([key_rot, value_low], 1)
    if paired:
        both_group = gather_pair([both], 2)[0]
    else:
        both_group = lax.all_gather(both, "shard", axis=0)
    both_group = both_group.reshape(shard_count, 2, sub_rows, 2 * kv_width)
    both_group = both_group.transpose(1, 0, 2, 3).reshape(2, seq_len, 2 * kv_width)
    allowed = (
        (own_positions[None, :, None] >= seq_positions[None, None, :])
        & (query_docs[:, :, None] == key_docs[:, None, :])
    )[:, None, None]
    query_heads = query_rot.reshape(2, sub_rows, KV_HEADS, group_ratio, HEAD_DIM)
    key_heads = both_group[:, :, :kv_width].reshape(2, seq_len, KV_HEADS, HEAD_DIM)
    value_heads = both_group[:, :, kv_width:].reshape(2, seq_len, KV_HEADS, HEAD_DIM)
    scores = (
        jnp.einsum("btkgd,bskd->bkgts", query_heads, key_heads, preferred_element_type=wide)
        * att_scale
    )
    scores = jnp.where(allowed, scores, masked_score)
    exp_scores = jnp.exp(scores - jnp.max(scores, -1, keepdims=True))
    probs = exp_scores / jnp.sum(exp_scores, -1, keepdims=True)
    probs_low = probs.astype(low)
    attn_mix = jnp.einsum("bkgts,bskd->btkgd", probs_low, value_heads, preferred_element_type=wide)
    attn_low = attn_mix.reshape(tok_count, -1).astype(low)
    branch = jnp.dot(attn_low, output_full, preferred_element_type=wide)
    middle = input_float + res_scale * branch
    normed_two = rms_norm(middle, moe_norm_gain).astype(low)
    send_rows, arrived_top = lax.optimization_barrier((to_slots(normed_two), arrived_top))
    arrived = cross(send_rows)

    def gate_softmax(rows, chosen):
        logits = jnp.dot(rows, router_full, preferred_element_type=wide)
        top = jnp.max(jnp.where(chosen, logits, -jnp.inf), -1, keepdims=True)
        top = jnp.where(jnp.any(chosen, -1, keepdims=True), top, 0.0)
        powers = jnp.where(chosen, jnp.exp(jnp.where(chosen, logits - top, 0.0)), 0.0)
        total = jnp.sum(powers, -1, keepdims=True)
        return powers / jnp.where(total > 0.0, total, 1.0)

    gates = gate_softmax(normed_two, picks)

    gate_matrix = gate_weight[0]
    up_matrix = up_weight[0]
    down_matrix = down_weight[0]
    flat_rows = arrived.reshape(-1, model_width)
    gate_pre = jnp.dot(flat_rows, gate_matrix, preferred_element_type=wide)
    up_pre = jnp.dot(flat_rows, up_matrix, preferred_element_type=wide)
    sigmoid_gate = jax.nn.sigmoid(gate_pre)
    activated = gate_pre * sigmoid_gate
    inner = (activated * up_pre).astype(low)
    result = jnp.dot(inner, down_matrix, preferred_element_type=wide).astype(low)

    flat_top = arrived_top.reshape(-1, arrived_top.shape[2])
    slot_picks = flat_top[:, model_width : model_width + expert_count] > 0.5
    slot_gates = gate_softmax(flat_rows, slot_picks)
    mine = jnp.arange(expert_count, dtype=jnp.int32)[None, :] == expert_index
    own_gate = jnp.sum(jnp.where(mine, slot_gates, 0.0), 1, keepdims=True)
    flat_grads = (own_gate * (res_scale * flat_top[:, :model_width].astype(wide))).astype(low)
    inner_grad = jnp.einsum("rd,fd->rf", flat_grads, down_matrix, preferred_element_type=wide)
    gate_pregrad = (
        inner_grad * up_pre * sigmoid_gate * (1.0 + gate_pre * (1.0 - sigmoid_gate))
    ).astype(low)
    up_pregrad = (inner_grad * activated).astype(low)
    row_grads = (
        jnp.einsum("rf,df->rd", gate_pregrad, gate_matrix, preferred_element_type=wide)
        + jnp.einsum("rf,df->rd", up_pregrad, up_matrix, preferred_element_type=wide)
    ).astype(low)
    slot_dots = res_scale * jnp.sum(
        flat_top[:, :model_width].astype(wide) * result.astype(wide), 1, keepdims=True
    )
    dots_high = slot_dots.astype(low)
    dots_rest = (slot_dots - dots_high.astype(wide)).astype(low)
    dots_both = jnp.pad(jnp.concatenate([dots_high, dots_rest], 1), ((0, 0), (0, 126)))
    row_grads = jnp.concatenate([row_grads, dots_both], 1)
    back_both = cross(row_grads.reshape(expert_axis, -1, row_grads.shape[1]))
    back_both = back_both.reshape(-1, row_grads.shape[1])
    down_wgrad = jnp.einsum("rf,rd->fd", inner, flat_grads, preferred_element_type=wide).astype(low)
    gate_wgrad = jnp.einsum(
        "rd,rf->df", flat_rows, gate_pregrad, preferred_element_type=wide
    ).astype(low)
    up_wgrad = jnp.einsum(
        "rd,rf->df", flat_rows, up_pregrad, preferred_element_type=wide
    ).astype(low)

    back_both, result, down_wgrad, gate_wgrad, up_wgrad = lax.optimization_barrier(
        (back_both, result, down_wgrad, gate_wgrad, up_wgrad)
    )
    returned = cross(result.reshape(expert_axis, -1, model_width)).reshape(-1, model_width)
    back_grads = back_both[:, :model_width]
    back_dots = jnp.sum(back_both[:, model_width : model_width + 2].astype(wide), 1, keepdims=True)
    grad_out = cotangent.astype(wide)
    picked_dots = hot.astype(wide) * back_dots
    grad_gates = jnp.sum(picked_dots.reshape(expert_count, capacity, tok_count), 1).T
    gate_dot = jnp.sum(gates * grad_gates, 1, keepdims=True)
    logit_grad = (gates * (grad_gates - gate_dot)).astype(low)
    router_wgrad = jnp.einsum("td,te->de", normed_two, logit_grad, preferred_element_type=wide)
    router_back = jnp.einsum("te,de->td", logit_grad, router_full, preferred_element_type=wide)
    normed_two_grad = (
        jnp.einsum("rt,rd->td", hot, back_grads, preferred_element_type=wide) + router_back
    )
    unused_value, second_pull = jax.vjp(rms_norm, middle, moe_norm_gain)
    middle_from_norm, moe_gain_grad = second_pull(normed_two_grad)
    middle_grad = grad_out + middle_from_norm
    branch_grad = (res_scale * middle_grad).astype(low)
    output_wgrad = jnp.einsum("tq,td->qd", attn_low, branch_grad, preferred_element_type=wide)
    attn_grad = jnp.einsum(
        "td,qd->tq", branch_grad, output_full, preferred_element_type=wide
    ).astype(low)
    attn_grad = attn_grad.reshape(2, sub_rows, KV_HEADS, group_ratio, HEAD_DIM)
    prob_grad = jnp.einsum("btkgd,bskd->bkgts", attn_grad, value_heads, preferred_element_type=wide)
    value_part = jnp.einsum("bkgts,btkgd->bskd", probs_low, attn_grad, preferred_element_type=wide)
    score_grad = (probs * (prob_grad - jnp.sum(probs * prob_grad, -1, keepdims=True))).astype(low)
    query_rot_grad = att_scale * jnp.einsum(
        "bkgts,bskd->btkgd", score_grad, key_heads, preferred_element_type=wide
    )
    key_part = att_scale * jnp.einsum(
        "bkgts,btkgd->bskd", score_grad, query_heads, preferred_element_type=wide
    )
    both_part = jnp.concatenate(
        [key_part.reshape(2, seq_len, -1), value_part.reshape(2, seq_len, -1)], -1
    ).astype(low)
    both_part = both_part.reshape(2, shard_count, sub_rows, 2 * kv_width).transpose(1, 0, 2, 3)
    both_part = both_part.reshape(shard_count, tok_count, 2 * kv_width)

    def own_block(values):
        return lax.dynamic_index_in_dim(values, shard_index, 0, keepdims=False).astype(wide)

    if paired:
        both_pre = own_block(both_part) + swap_pair(both_part, 3).astype(wide)
    else:
        both_pre = lax.psum_scatter(both_part, "shard", scatter_dimension=0).astype(wide)
    query_pre_grad = rotate(
        query_rot_grad.reshape(tok_count, -1), cos_table, sin_table, True
    ).astype(low)
    key_pre_grad = rotate(both_pre[:, :kv_width], cos_table, sin_table, True).astype(low)
    value_pre_grad = both_pre[:, kv_width:].astype(low)
    both_pre_grad = jnp.concatenate([key_pre_grad, value_pre_grad], 1)
    query_wgrad = jnp.einsum("td,tq->dq", normed_one, query_pre_grad, preferred_element_type=wide)
    both_wgrad = jnp.einsum("td,tq->dq", normed_one, both_pre_grad, preferred_element_type=wide)
    normed_one_grad = (
        jnp.einsum("tq,dq->td", query_pre_grad, query_full, preferred_element_type=wide)
        + jnp.einsum("tq,dq->td", key_pre_grad, key_full, preferred_element_type=wide)
        + jnp.einsum("tq,dq->td", value_pre_grad, value_full, preferred_element_type=wide)
    )
    unused_first, first_pull = jax.vjp(rms_norm, input_float, attn_norm_gain)
    input_from_norm, attn_gain_grad = first_pull(normed_one_grad)
    input_grad = middle_grad + input_from_norm

    gates_slots = jnp.repeat(gates.T, capacity, 0) * hot.astype(wide)
    gates_high = gates_slots.astype(low)
    gates_rest = (gates_slots - gates_high.astype(wide)).astype(low)
    mixture = jnp.einsum(
        "rt,rd->td", gates_high, returned, preferred_element_type=wide
    ) + jnp.einsum("rt,rd->td", gates_rest, returned, preferred_element_type=wide)
    layer_out = (middle + res_scale * mixture).astype(low)

    small = jnp.concatenate(
        [router_wgrad, attn_gain_grad[:, None], moe_gain_grad[:, None]], 1
    ).astype(low)
    small = jnp.pad(small, ((0, 0), (0, -small.shape[1] % 128)))
    batch_sums = [query_wgrad.astype(low), output_wgrad.astype(low), both_wgrad.astype(low), small]
    expert_parts = [
        a.reshape(shard_count, -1, a.shape[1]) for a in (gate_wgrad, up_wgrad, down_wgrad)
    ]
    whole_rows = model_width // shard_count
    if paired and expert_axis & (expert_axis - 1) == 0 and whole_rows % (16 * expert_axis) == 0:
        reduced = reduce_all(batch_sums, expert_parts, expert_axis, 4)
        totals = [a.astype(wide) for a in reduced[:4]]
        expert_sums = [
            own_block(own) + got.astype(wide) for own, got in zip(expert_parts, reduced[4:])
        ]
    else:
        totals = []
        for array in batch_sums:
            part = lax.psum_scatter(array, "shard", scatter_dimension=0, tiled=True)
            totals.append(lax.psum(part, "expert").astype(wide))
        expert_sums = [
            lax.psum_scatter(a, "shard", scatter_dimension=0).astype(wide) for a in expert_parts
        ]
    return (
        layer_out,
        input_grad,
        totals[3][:, expert_count],
        totals[0],
        totals[2][:, :kv_width],
        totals[2][:, kv_width:],
        totals[1],
        totals[3][:, :expert_count],
        totals[3][:, expert_count + 1],
        expert_sums[0][None],
        expert_sums[1][None],
        expert_sums[2][None],
    )


def solution(mesh):
    return jax.shard_map(
        on_device,
        mesh=mesh,
        in_specs=(
            P(("expert", "shard"), None),
            P("expert", None),
            P(("expert", "shard"), None),
            P(),
            P("shard", None),
            P("shard", None),
            P("shard", None),
            P("shard", None),
            P("shard", None),
            P(),
            P("expert", None, None),
            P("expert", None, None),
            P("expert", None, None),
            P(("expert", "shard"), None),
        ),
        out_specs=(
            P(("expert", "shard"), None),
            P(("expert", "shard"), None),
            P("shard"),
            P("shard", None),
            P("shard", None),
            P("shard", None),
            P("shard", None),
            P("shard", None),
            P("shard"),
            P("expert", "shard", None),
            P("expert", "shard", None),
            P("expert", "shard", None),
        ),
        check_vma=False,
    )
```
